32 devices in a mesh: row: 2 (over core), col: 16 (over z, y, x).
Axes of the slice: x: 2, y: 2, z: 4, core: 2. Of those that a mesh axis runs over, the one named last changes fastest.
Arguments:
- node_latent: float32 [3072, 512], P(('row', 'col')), may hold values from -6 to 6
- edge_latent: bfloat16 [65536, 512], P(('row', 'col')), may hold values from -6 to 6
- senders: int32 [65536], P(('row', 'col')), may hold values from 0 to 3071, as said below
- receivers: int32 [65536], P(('row', 'col')), may hold values from 0 to 3071, as said below
- edge_count: int32 [32], P(('row', 'col')), may hold values from 512 to 2048, as said below
- edge_in: bfloat16 [2, 1536, 512], replicated, may hold values from -0.15625 to 0.15625
- edge_out: bfloat16 [2, 512, 512], replicated
- node_in: bfloat16 [2, 1024, 512], replicated, may hold values from -0.1875 to 0.1875
- node_out: bfloat16 [2, 512, 512], replicated
Outputs:
- updated_nodes: float32 [3072, 512], P(('row', 'col'))
The draws below stay inside these ranges and needn't reach their ends.
Inputs may be any that keep to these rules, and one draw needn't show every extreme that they name: `senders`: the sender of every slot of tile t lies in sender patch t // 16. `receivers`: the receiver of every slot of tile t lies in receiver patch t % 16. Slots that are not live hold ids of the same patches. `edge_count`: some tile is full.
All inputs are finite; a program needn't handle non-finite values.
Results may differ from the reference program's by a relative error of at most 0.011.
Values may be sent and summed in bfloat16 or wider, within the bound.
A program may use at most 128 MiB of HBM per device.

```python
import jax
import jax.numpy as jnp
from jax import lax

D = 512
NODE_DEV = 96
LAYERS = 2
CAP = 2048
SEND_PATCHES = 2
RECV_PATCHES = 16
TILES = 32
SPATCH = 1536
NODES = 3072


def draw_senders(key, part):
    key = jax.random.fold_in(key, 11)
    slot_index = jnp.arange(TILES * CAP, dtype=jnp.int32)
    patch_index = slot_index // CAP // RECV_PATCHES
    offsets = jax.random.randint(key, (TILES * CAP,), 0, SPATCH, dtype=jnp.int32)
    node_ids = patch_index * SPATCH + offsets
    node_ids = jnp.where(slot_index == 0, 0, node_ids)
    node_ids = jnp.where(slot_index == TILES * CAP - 1, NODES - 1, node_ids)
    return node_ids


def draw_receivers(key, part):
    key = jax.random.fold_in(key, 12)
    key_patch, key_node = jax.random.split(key)
    slot_index = jnp.arange(TILES * CAP, dtype=jnp.int32)
    patch_index = slot_index // CAP % RECV_PATCHES
    sender_part = jax.random.randint(key_patch, (TILES * CAP,), 0, SEND_PATCHES, dtype=jnp.int32)
    inner = jax.random.randint(key_node, (TILES * CAP,), 0, NODE_DEV, dtype=jnp.int32)
    node_ids = sender_part * SPATCH + patch_index * NODE_DEV + inner
    node_ids = jnp.where(slot_index == 0, 0, node_ids)
    node_ids = jnp.where(slot_index == TILES * CAP - 1, NODES - 1, node_ids)
    return node_ids


def draw_edge_count(key, part):
    key = jax.random.fold_in(key, 13)
    key_count, key_full, key_least = jax.random.split(key, 3)
    counts = jax.random.randint(key_count, (TILES,), CAP // 4, CAP, dtype=jnp.int32)
    tile_index = jnp.arange(TILES, dtype=jnp.int32)
    full_tile = jax.random.randint(key_full, (), 0, TILES, dtype=jnp.int32)
    least_tile = (full_tile + 1 + jax.random.randint(key_least, (), 0, TILES - 1, dtype=jnp.int32)) % TILES
    counts = jnp.where(tile_index == full_tile, CAP, counts)
    counts = jnp.where(tile_index == least_tile, CAP // 4, counts)
    return counts


def draw_edge_out(key, part):
    key = jax.random.fold_in(key, 21)
    base_key, scale_key = jax.random.split(key)
    base = jax.random.normal(base_key, (LAYERS, D, D), jnp.float32)
    scales = jnp.exp(jax.random.uniform(scale_key, (LAYERS, 1, D), jnp.float32, 0.0, 2.3025851))
    return (base * scales * D ** (-0.5)).astype(jnp.bfloat16)


def draw_node_out(key, part):
    key = jax.random.fold_in(key, 22)
    base_key, scale_key = jax.random.split(key)
    base = jax.random.normal(base_key, (LAYERS, D, D), jnp.float32)
    scales = jnp.exp(jax.random.uniform(scale_key, (LAYERS, 1, D), jnp.float32, 0.0, 2.3025851))
    return (base * scales * D ** (-0.5)).astype(jnp.bfloat16)


def level_of(stream_key, dims, pieces, low, largest):
    loudness, own = 1.0, jax.random.fold_in(stream_key, 6)
    for dim, shards_of in pieces:
        steps = jnp.exp(jax.random.uniform(jax.random.fold_in(own, dim), (shards_of,), jnp.float32, low / len(pieces), largest / len(pieces)))
        loudness = loudness * jnp.repeat(steps, dims[dim] // shards_of).reshape([-1 if axis == dim else 1 for axis in range(len(dims))])
    return loudness


def noise(stream_key, extent, deviation, reach, cuts=(), kind=jnp.bfloat16):
    drawn = jax.random.normal(stream_key, extent, jnp.float32) * deviation
    if len(cuts) > 0:
        drawn = level_of(stream_key, extent, cuts, -0.22, 0.18) * drawn
    return jnp.clip(drawn, min=-reach, max=reach).astype(kind)


def setup_inputs(seed: int = 0) -> dict:
    keys = jax.random.split(jax.random.key(seed), 10)
    node_latent = noise(keys[0], (NODES, D), 1.0, 6.0, ((0, 32),), jnp.float32)
    edge_latent = noise(keys[1], (TILES * CAP, D), 1.0, 6.0, ((0, 32),))
    senders = draw_senders(jax.random.fold_in(keys[9], 71), 0)
    receivers = draw_receivers(jax.random.fold_in(keys[9], 71), 0)
    edge_count = draw_edge_count(jax.random.fold_in(keys[9], 71), 0)
    edge_in = noise(keys[5], (LAYERS, 3 * D, D), (3 * D) ** -0.5, 0.15625)
    edge_out = draw_edge_out(jax.random.fold_in(keys[9], 71), 0)
    node_in = noise(keys[7], (LAYERS, 2 * D, D), (2 * D) ** -0.5, 0.1875)
    node_out = draw_node_out(jax.random.fold_in(keys[9], 71), 0)
    return {"node_latent": node_latent, "edge_latent": edge_latent, "senders": senders, "receivers": receivers, "edge_count": edge_count, "edge_in": edge_in, "edge_out": edge_out, "node_in": node_in, "node_out": node_out}


def layer_norm(values):
    centre = values - lax.optimization_barrier(jnp.mean(values, axis=-1, keepdims=True))
    spread = lax.optimization_barrier(jnp.mean(centre * centre, axis=-1, keepdims=True))
    return centre * lax.rsqrt(spread + 1e-05)

def reference(node_latent, edge_latent, senders, receivers, edge_count, edge_in, edge_out, node_in, node_out):
    node_state = node_latent
    edge_state = edge_latent.astype(jnp.float32).reshape(TILES, CAP, D)
    send_tiles = senders.reshape(TILES, CAP)
    receive_tiles = receivers.reshape(TILES, CAP)
    live_mask = jnp.arange(CAP, dtype=jnp.int32)[None, :] < edge_count[:, None]
    for layer_id in range(LAYERS):
        w_edge_in = edge_in[layer_id]
        w_edge_out = edge_out[layer_id]
        node_half = node_state.astype(jnp.bfloat16)
        send_table = jnp.dot(node_half, w_edge_in[D:2 * D], preferred_element_type=jnp.float32)
        receive_table = jnp.dot(node_half, w_edge_in[2 * D:], preferred_element_type=jnp.float32)

        def tile_update(tile_items):
            edge_tile, send_ids, receive_ids = tile_items
            first_out = jnp.dot(edge_tile.astype(jnp.bfloat16), w_edge_in[:D], preferred_element_type=jnp.float32)
            first_out = first_out + send_table[send_ids] + receive_table[receive_ids]
            hidden = jax.nn.silu(first_out).astype(jnp.bfloat16)
            return edge_tile + layer_norm(jnp.dot(hidden, w_edge_out, preferred_element_type=jnp.float32))
        edge_state = lax.map(tile_update, (edge_state, send_tiles, receive_tiles))
        masked = jnp.where(live_mask[:, :, None], edge_state, 0.0)
        edge_total = jax.ops.segment_sum(masked.reshape(TILES * CAP, D), receivers, num_segments=NODES)
        joined = jnp.concatenate([node_half, edge_total.astype(jnp.bfloat16)], axis=1)
        hidden = jax.nn.silu(jnp.dot(joined, node_in[layer_id], preferred_element_type=jnp.float32)).astype(jnp.bfloat16)
        node_state = node_state + layer_norm(jnp.dot(hidden, node_out[layer_id], preferred_element_type=jnp.float32))
    return node_state
```

```python
import functools

import jax
import jax.numpy as jnp
from jax import lax
from jax.experimental import pallas as pl
from jax.experimental.pallas import tpu as pltpu
from jax.sharding import PartitionSpec as P

MESH = pl.DeviceIdType.MESH
HALVES = 2
EDGE_ROWS = 256


def layer_norm(values):
    centre = values - jnp.mean(values, axis=-1, keepdims=True)
    spread = jnp.mean(centre * centre, axis=-1, keepdims=True)
    return centre * lax.rsqrt(spread + 1e-05)


def product(matrix, weight):
    return jnp.dot(matrix, weight, preferred_element_type=jnp.float32)


def silu(values):
    half = 0.5 * values
    return half + half * jnp.tanh(half)


def kernel(
    lines,
    ids_ref,
    receive_row_ref,
    node_hbm,
    edge_hbm,
    edge_in_hbm,
    edge_out_hbm,
    node_in_hbm,
    node_out_hbm,
    out_ref,
    node_state,
    edge_half,
    edge_state,
    acc,
    onehot,
    scatter_hot,
    table,
    w_edge_in,
    w_edge_out,
    w_node_in,
    w_node_out,
    partial_sum,
    part_out,
    part_in,
    node_first,
    load_sem,
    gather_send,
    gather_recv,
    row_send,
    row_recv,
    part_send,
    part_recv,
):
    layers, _, width = w_edge_in.shape
    own = node_state.shape[0]
    slots = edge_half.shape[0]
    rows = part_in.shape[1] + 1
    piece = own // HALVES
    group = HALVES * lines * piece
    send_rows = 4 * group
    recv_rows = rows * own
    tiles = slots // EDGE_ROWS

    row_me = lax.axis_index("row")
    col_me = lax.axis_index("col")
    a_me = col_me // 4
    inner = lax.rem(col_me, 4)
    b_me = inner // 2
    c_me = lax.rem(inner, 2)
    flip_b = a_me * 4 + (1 - b_me) * 2 + c_me
    flip_c = a_me * 4 + b_me * 2 + (1 - c_me)

    def line_peer(step):
        return lax.rem(a_me + lines - step, lines) * 4 + inner

    def row_peer(step):
        return lax.rem(row_me + rows + step, rows)

    barrier = pltpu.get_barrier_semaphore()
    for step in range(1, lines):
        pl.semaphore_signal(barrier, inc=1, device_id={"col": line_peer(step)}, device_id_type=MESH)
    for target in (flip_b, flip_c):
        pl.semaphore_signal(barrier, inc=1, device_id={"col": target}, device_id_type=MESH)
    for step in range(1, rows):
        pl.semaphore_signal(barrier, inc=1, device_id={"row": row_peer(step)}, device_id_type=MESH)

    loads = {}

    def load(name, source, target):
        copy = pltpu.make_async_copy(source, target, load_sem.at[len(loads)])
        copy.start()
        loads[name] = copy

    load("node", node_hbm, node_state)
    for layer_id in range(layers):
        for name, part in (("send", 1), ("receive", 2), ("edge", 0)):
            span = pl.ds(part * width, width)
            load(
                (name, layer_id),
                edge_in_hbm.at[layer_id, span],
                w_edge_in.at[layer_id, span],
            )
            if layer_id == 0 and name == "receive":
                load("edges", edge_hbm, edge_half)
        load(("node_in", layer_id), node_in_hbm.at[layer_id], w_node_in.at[layer_id])
        load(("edge_out", layer_id), edge_out_hbm.at[layer_id], w_edge_out.at[layer_id])
        load(("node_out", layer_id), node_out_hbm.at[layer_id], w_node_out.at[layer_id])

    def slot_row(half, slot):
        kind, line = slot // lines, slot % lines
        return kind * group + half * lines * piece + line * piece

    pending = []
    loads["node"].wait()
    for layer_id in range(layers):
        copies = {}

        def push(half, source, slot, target, layer_id=layer_id, copies=copies):
            copy = pltpu.make_async_remote_copy(
                src_ref=table.at[layer_id, pl.ds(slot_row(half, source), piece)],
                dst_ref=table.at[layer_id, pl.ds(slot_row(half, slot), piece)],
                send_sem=gather_send.at[layer_id, half, slot],
                recv_sem=gather_recv.at[layer_id, half, slot],
                device_id={"col": target},
                device_id_type=MESH,
            )
            copy.start()
            copies[half, slot] = copy
            pending.append(copy)

        first_target = (flip_c, flip_b)
        second_target = (flip_b, flip_c)
        w_edge = w_edge_in.at[layer_id]
        node_half = node_state[...].astype(jnp.bfloat16)

        loads["send", layer_id].wait()
        sent = product(node_half, w_edge[width : 2 * width, :]).astype(jnp.bfloat16)
        for half in range(HALVES):
            table[layer_id, pl.ds(slot_row(half, 0), piece), :] = sent[
                half * piece : (half + 1) * piece
            ]
        if layer_id == 0:
            pl.semaphore_wait(barrier, lines - 1 + 2 + rows - 1)
        for half in range(HALVES):
            push(half, 0, lines, first_target[half])
        for step in range(1, lines):
            for half in range(HALVES):
                push(half, 0, step, line_peer(step))
        for half in range(HALVES):
            push(half, 0, 2 * lines, second_target[half])

        loads["receive", layer_id].wait()
        table[layer_id, pl.ds(send_rows, own), :] = product(
            node_half, w_edge[2 * width : 3 * width, :]
        ).astype(jnp.bfloat16)
        row_copies = []
        for step in range(1, rows):
            copy = pltpu.make_async_remote_copy(
                src_ref=table.at[layer_id, pl.ds(send_rows, own)],
                dst_ref=table.at[layer_id, pl.ds(send_rows + step * own, own)],
                send_sem=row_send.at[layer_id, step - 1],
                recv_sem=row_recv.at[layer_id, step - 1],
                device_id={"row": row_peer(-step)},
                device_id_type=MESH,
            )
            copy.start()
            row_copies.append(copy)
            pending.append(copy)

        loads["node_in", layer_id].wait()
        node_first[...] = product(node_half, w_node_in[layer_id, :width, :])

        loads["edge", layer_id].wait()
        if layer_id == 0:
            loads["edges"].wait()

        def early(tile, carry, layer_id=layer_id, w_edge=w_edge):
            span = pl.ds(pl.multiple_of(tile * EDGE_ROWS, EDGE_ROWS), EDGE_ROWS)
            acc[span, :] = product(edge_half[span, :], w_edge[:width, :])
            if layer_id == 0:
                ids = ids_ref[span, :]
                send_lane = lax.broadcasted_iota(jnp.int32, (EDGE_ROWS, send_rows), 1)
                onehot[span, :send_rows] = jnp.where(send_lane == ids[:, 0:1], 1.0, 0.0).astype(
                    jnp.bfloat16
                )
                recv_lane = lax.broadcasted_iota(jnp.int32, (EDGE_ROWS, recv_rows), 1)
                onehot[span, send_rows:] = jnp.where(recv_lane == ids[:, 1:2], 1.0, 0.0).astype(
                    jnp.bfloat16
                )
            return carry

        def forward_line(step):
            for half in range(HALVES):
                copies[half, step].wait_recv()
                push(half, step, lines + step, first_target[half])
                push(half, step, 2 * lines + step, second_target[half])

        def forward_first(step):
            for half in range(HALVES):
                copies[half, lines + step].wait_recv()
                push(half, lines + step, 3 * lines + step, second_target[half])

        middle_tile = tiles // 2
        lax.fori_loop(0, middle_tile, early, 0)
        forward_first(0)
        forward_line(1)
        lax.fori_loop(middle_tile, tiles, early, 0)
        if layer_id == 0:
            slot_id = lax.broadcasted_iota(jnp.int32, (recv_rows, slots), 0)
            scatter_hot[...] = jnp.where(slot_id == receive_row_ref[...], 1.0, 0.0).astype(
                jnp.bfloat16
            )
        for step in range(2, lines):
            forward_line(step)
        for step in range(1, lines):
            forward_first(step)
        for copy in row_copies:
            copy.wait_recv()

        def middle(tile, carry, layer_id=layer_id):
            span = pl.ds(pl.multiple_of(tile * EDGE_ROWS, EDGE_ROWS), EDGE_ROWS)
            acc[span, :] += product(
                onehot[span, : 2 * group], table[layer_id, : 2 * group, :]
            ) + product(onehot[span, send_rows:], table[layer_id, send_rows:, :])
            return carry

        lax.fori_loop(0, tiles, middle, 0)
        for step in range(2 * lines):
            for half in range(HALVES):
                copies[half, 2 * lines + step].wait_recv()

        loads["edge_out", layer_id].wait()
        partial_sum[...] = jnp.zeros_like(partial_sum)

        def late(tile, carry, layer_id=layer_id):
            span = pl.ds(pl.multiple_of(tile * EDGE_ROWS, EDGE_ROWS), EDGE_ROWS)
            first_out = acc[span, :] + product(
                onehot[span, 2 * group : send_rows], table[layer_id, 2 * group : send_rows, :]
            )
            hidden = silu(first_out).astype(jnp.bfloat16)
            if layer_id == 0:
                before = edge_half[span, :].astype(jnp.float32)
            else:
                before = edge_state[span, :]
            after = before + layer_norm(product(hidden, w_edge_out[layer_id]))
            after_half = after.astype(jnp.bfloat16)
            if layer_id < layers - 1:
                edge_state[span, :] = after
                edge_half[span, :] = after_half
            partial_sum[...] += product(scatter_hot[:, span], after_half)
            return carry

        lax.fori_loop(0, tiles, late, 0)

        part_copies = []
        for step in range(1, rows):
            part_out[layer_id, step - 1] = partial_sum[
                step * own : (step + 1) * own, :
            ].astype(jnp.bfloat16)
            copy = pltpu.make_async_remote_copy(
                src_ref=part_out.at[layer_id, step - 1],
                dst_ref=part_in.at[layer_id, step - 1],
                send_sem=part_send.at[layer_id, step - 1],
                recv_sem=part_recv.at[layer_id, step - 1],
                device_id={"row": row_peer(step)},
                device_id_type=MESH,
            )
            copy.start()
            part_copies.append(copy)
            pending.append(copy)
        edge_total = partial_sum[:own, :]
        for step, copy in enumerate(part_copies):
            copy.wait_recv()
            edge_total = edge_total + part_in[layer_id, step].astype(jnp.float32)

        loads["node_out", layer_id].wait()
        first_out = node_first[...] + product(
            edge_total.astype(jnp.bfloat16), w_node_in[layer_id, width:, :]
        )
        hidden = silu(first_out).astype(jnp.bfloat16)
        after = node_state[...] + layer_norm(product(hidden, w_node_out[layer_id]))
        if layer_id < layers - 1:
            node_state[...] = after
        else:
            out_ref[...] = after
    for copy in pending:
        copy.wait_send()


def per_device(
    node_latent, edge_latent, senders, receivers, edge_count, edge_in, edge_out, node_in, node_out
):
    own, width = node_latent.shape
    slots = edge_latent.shape[0]
    layers = edge_in.shape[0]
    cols = lax.axis_size("col")
    rows = lax.axis_size("row")
    lines = cols // 4
    piece = own // HALVES
    row_me = lax.axis_index("row")
    col_me = lax.axis_index("col")
    send_patch = own * cols
    local = senders - row_me * send_patch
    block, offset = local // own, local % own
    line = (block // 4 - col_me // 4) % lines
    flip_b = (block // 2 % 2) ^ (col_me // 2 % 2)
    flip_c = (block % 2) ^ (col_me % 2)
    half = offset // piece
    first = jnp.where(half == 0, flip_c, flip_b)
    second = jnp.where(half == 0, flip_b, flip_c)
    send_slot = (
        (second * 2 + first) * (HALVES * lines * piece)
        + half * (lines * piece)
        + line * piece
        + offset % piece
    )
    receive_slot = (receivers // send_patch - row_me) % rows * own + receivers % own
    ids = jnp.stack([send_slot, receive_slot], axis=1)
    live_mask = jnp.arange(slots, dtype=jnp.int32) < edge_count[0]
    receive_row = jnp.where(live_mask, receive_slot, -1)[None, :]

    send_rows, recv_rows = cols * own, rows * own
    half_type, full_type = jnp.bfloat16, jnp.float32
    vmem = pl.BlockSpec(memory_space=pltpu.VMEM)
    anywhere = pl.BlockSpec(memory_space=pl.ANY)
    dma = pltpu.SemaphoreType.DMA
    return pl.pallas_call(
        functools.partial(kernel, lines),
        out_shape=jax.ShapeDtypeStruct((own, width), full_type),
        in_specs=[vmem] * 2 + [anywhere] * 6,
        out_specs=vmem,
        scratch_shapes=[
            pltpu.VMEM((own, width), full_type),
            pltpu.VMEM((slots, width), half_type),
            pltpu.VMEM((slots, width), full_type),
            pltpu.VMEM((slots, width), full_type),
            pltpu.VMEM((slots, send_rows + recv_rows), half_type),
            pltpu.VMEM((recv_rows, slots), half_type),
            pltpu.VMEM((layers, send_rows + recv_rows, width), half_type),
            pltpu.VMEM(edge_in.shape, half_type),
            pltpu.VMEM(edge_out.shape, half_type),
            pltpu.VMEM(node_in.shape, half_type),
            pltpu.VMEM(node_out.shape, half_type),
            pltpu.VMEM((recv_rows, width), full_type),
            pltpu.VMEM((layers, rows - 1, own, width), half_type),
            pltpu.VMEM((layers, rows - 1, own, width), half_type),
            pltpu.VMEM((own, width), full_type),
            dma((2 + 6 * layers,)),
            dma((layers, HALVES, cols)),
            dma((layers, HALVES, cols)),
            dma((layers, rows - 1)),
            dma((layers, rows - 1)),
            dma((layers, rows - 1)),
            dma((layers, rows - 1)),
        ],
        compiler_params=pltpu.CompilerParams(
            collective_id=0, has_side_effects=True, vmem_limit_bytes=60 * 1024 * 1024
        ),
    )(ids, receive_row, node_latent, edge_latent, edge_in, edge_out, node_in, node_out)


def solution(mesh):
    placed = (
        P(("row", "col"), None),
        P(("row", "col"), None),
        P(("row", "col")),
        P(("row", "col")),
        P(("row", "col")),
        P(),
        P(),
        P(),
        P(),
    )
    return jax.shard_map(
        per_device, mesh=mesh, in_specs=placed, out_specs=P(("row", "col"), None), check_vma=False
    )
```

```python
import functools

import jax
import jax.numpy as jnp
from jax import lax
from jax.experimental import pallas as pl
from jax.experimental.pallas import tpu as pltpu
from jax.sharding import PartitionSpec as P

MESH = pl.DeviceIdType.MESH
HALVES = 2
EDGE_ROWS = 1024
CHUNK = 128


def layer_norm(values):
    centre = values - jnp.mean(values, axis=-1, keepdims=True)
    spread = jnp.mean(centre * centre, axis=-1, keepdims=True)
    return centre * lax.rsqrt(spread + 1e-05)


def product(matrix, weight):
    return jnp.dot(matrix, weight, preferred_element_type=jnp.float32)


def silu(values):
    half = 0.5 * values
    return half + half * jnp.tanh(half)


def kernel(
    lines,
    count_ref,
    senders_ref,
    receivers_ref,
    node_hbm,
    edge_hbm,
    edge_in_hbm,
    edge_out_hbm,
    node_in_hbm,
    node_out_hbm,
    out_ref,
    node_state,
    edge_half,
    edge_state,
    acc,
    onehot,
    scatter_hot,
    table,
    w_edge_in,
    w_edge_out,
    w_node_in,
    w_node_out,
    partial_sum,
    part_out,
    part_in,
    node_first,
    places,
    load_sem,
    gather_send,
    gather_recv,
    row_send,
    row_recv,
    part_send,
    part_recv,
):
    layers, _, width = w_edge_in.shape
    own = node_state.shape[0]
    slots = edge_half.shape[0]
    rows = part_in.shape[1] + 1
    piece = own // HALVES
    group = HALVES * lines * piece
    send_rows = 4 * group
    recv_rows = rows * own
    tiles = slots // EDGE_ROWS

    row_me = lax.axis_index("row")
    col_me = lax.axis_index("col")
    a_me = col_me // 4
    inner = lax.rem(col_me, 4)
    b_me = inner // 2
    c_me = lax.rem(inner, 2)
    flip_b = a_me * 4 + (1 - b_me) * 2 + c_me
    flip_c = a_me * 4 + b_me * 2 + (1 - c_me)

    def line_peer(step):
        return lax.rem(a_me + lines - step, lines) * 4 + inner

    def row_peer(step):
        return lax.rem(row_me + rows + step, rows)

    barrier = pltpu.get_barrier_semaphore()
    for step in range(1, lines):
        pl.semaphore_signal(barrier, inc=1, device_id={"col": line_peer(step)}, device_id_type=MESH)
    for target in (flip_b, flip_c):
        pl.semaphore_signal(barrier, inc=1, device_id={"col": target}, device_id_type=MESH)
    for step in range(1, rows):
        pl.semaphore_signal(barrier, inc=1, device_id={"row": row_peer(step)}, device_id_type=MESH)

    loads = {}

    def load(name, source, target):
        copy = pltpu.make_async_copy(source, target, load_sem.at[len(loads)])
        copy.start()
        loads[name] = copy

    def load_edge_in(layer_id, name, part):
        span = pl.ds(part * width, width)
        load((name, layer_id), edge_in_hbm.at[layer_id, span], w_edge_in.at[layer_id, span])

    def load_rest():
        for layer_id in range(layers):
            if layer_id > 0:
                load_edge_in(layer_id, "send", 1)
            load_edge_in(layer_id, "receive", 2)
            load(("node_in", layer_id), node_in_hbm.at[layer_id], w_node_in.at[layer_id])
            load_edge_in(layer_id, "edge", 0)
            if layer_id == 0:
                load("edges", edge_hbm, edge_half)
            load(("edge_out", layer_id), edge_out_hbm.at[layer_id], w_edge_out.at[layer_id])
            load(("node_out", layer_id), node_out_hbm.at[layer_id], w_node_out.at[layer_id])

    load("node", node_hbm, node_state)
    load_edge_in(0, "send", 1)

    def floor_part(values, size):
        return jnp.floor((values + 0.5) * (1.0 / size))

    def place_edges():
        local = (senders_ref[...] - row_me * (own * 4 * lines)).astype(jnp.float32)
        block = floor_part(local, own)
        offset = local - block * own
        line = floor_part(block, 4)
        corner = block - line * 4
        corner_b = floor_part(corner, 2)
        line = line - a_me.astype(jnp.float32)
        line = jnp.where(line < 0.0, line + lines, line)
        flipped_b = jnp.abs(corner_b - b_me.astype(jnp.float32))
        flipped_c = jnp.abs(corner - corner_b * 2 - c_me.astype(jnp.float32))
        half = floor_part(offset, piece)
        first = jnp.where(half == 0.0, flipped_c, flipped_b)
        second = jnp.where(half == 0.0, flipped_b, flipped_c)
        places[0:1, :] = (
            (second * 2 + first) * group
            + half * (lines * piece)
            + line * piece
            + (offset - half * piece)
        )
        receiver = receivers_ref[...].astype(jnp.float32)
        patch = floor_part(receiver, own * 4 * lines)
        inside = receiver - patch * (own * 4 * lines)
        inside = inside - floor_part(inside, own) * own
        patch = patch - row_me.astype(jnp.float32)
        patch = jnp.where(patch < 0.0, patch + rows, patch)
        places[1:2, :] = patch * own + inside

    place_edges()

    def slot_row(half, slot):
        kind, line = slot // lines, slot % lines
        return kind * group + half * lines * piece + line * piece

    pending = []
    loads["node"].wait()
    for layer_id in range(layers):
        copies = {}

        def push(half, source, slot, target, layer_id=layer_id, copies=copies):
            copy = pltpu.make_async_remote_copy(
                src_ref=table.at[layer_id, pl.ds(slot_row(half, source), piece)],
                dst_ref=table.at[layer_id, pl.ds(slot_row(half, slot), piece)],
                send_sem=gather_send.at[layer_id, half, slot],
                recv_sem=gather_recv.at[layer_id, half, slot],
                device_id={"col": target},
                device_id_type=MESH,
            )
            copy.start()
            copies[half, slot] = copy
            pending.append(copy)

        first_target = (flip_c, flip_b)
        second_target = (flip_b, flip_c)
        w_edge = w_edge_in.at[layer_id]
        node_half = node_state[...].astype(jnp.bfloat16)

        loads["send", layer_id].wait()
        sent = product(node_half, w_edge[width : 2 * width, :]).astype(jnp.bfloat16)
        for half in range(HALVES):
            table[layer_id, pl.ds(slot_row(half, 0), piece), :] = sent[
                half * piece : (half + 1) * piece
            ]
        if layer_id == 0:
            pl.semaphore_wait(barrier, lines - 1 + 2 + rows - 1)
        for half in range(HALVES):
            push(half, 0, lines, first_target[half])
        for step in range(1, lines):
            for half in range(HALVES):
                push(half, 0, step, line_peer(step))
        for half in range(HALVES):
            push(half, 0, 2 * lines, second_target[half])
        if layer_id == 0:
            load_rest()

        loads["receive", layer_id].wait()
        table[layer_id, pl.ds(send_rows, own), :] = product(
            node_half, w_edge[2 * width : 3 * width, :]
        ).astype(jnp.bfloat16)
        row_copies = []
        for step in range(1, rows):
            copy = pltpu.make_async_remote_copy(
                src_ref=table.at[layer_id, pl.ds(send_rows, own)],
                dst_ref=table.at[layer_id, pl.ds(send_rows + step * own, own)],
                send_sem=row_send.at[layer_id, step - 1],
                recv_sem=row_recv.at[layer_id, step - 1],
                device_id={"row": row_peer(-step)},
                device_id_type=MESH,
            )
            copy.start()
            row_copies.append(copy)
            pending.append(copy)

        loads["node_in", layer_id].wait()
        node_first[...] = product(node_half, w_node_in[layer_id, :width, :])

        loads["edge", layer_id].wait()
        if layer_id == 0:
            loads["edges"].wait()

        def early(tile, carry, layer_id=layer_id, w_edge=w_edge):
            span = pl.ds(pl.multiple_of(tile * EDGE_ROWS, EDGE_ROWS), EDGE_ROWS)
            acc[span, :] = product(edge_half[span, :], w_edge[:width, :])
            if layer_id == 0:
                diagonal = lax.broadcasted_iota(
                    jnp.int32, (CHUNK, CHUNK), 0
                ) == lax.broadcasted_iota(jnp.int32, (CHUNK, CHUNK), 1)
                for chunk in range(EDGE_ROWS // CHUNK):
                    part = pl.ds(
                        pl.multiple_of(tile * EDGE_ROWS + chunk * CHUNK, CHUNK), CHUNK
                    )
                    for place, low, high in (
                        (0, 0, send_rows),
                        (1, send_rows, send_rows + recv_rows),
                    ):
                        column = jnp.sum(
                            jnp.where(diagonal, places[place : place + 1, part], 0.0),
                            axis=1,
                            keepdims=True,
                        ).astype(jnp.int32)
                        lane = lax.broadcasted_iota(jnp.int32, (CHUNK, high - low), 1)
                        onehot[part, low:high] = jnp.where(lane == column, 1.0, 0.0).astype(
                            jnp.bfloat16
                        )
            return carry

        def forward_line(step):
            for half in range(HALVES):
                copies[half, step].wait_recv()
                push(half, step, lines + step, first_target[half])
                push(half, step, 2 * lines + step, second_target[half])

        def forward_first(step):
            for half in range(HALVES):
                copies[half, lines + step].wait_recv()
                push(half, lines + step, 3 * lines + step, second_target[half])

        middle_tile = tiles // 2
        lax.fori_loop(0, middle_tile, early, 0)
        forward_first(0)
        forward_line(1)
        lax.fori_loop(middle_tile, tiles, early, 0)
        if layer_id == 0:
            slot_id = lax.broadcasted_iota(jnp.int32, (recv_rows, slots), 0)
            live = lax.broadcasted_iota(jnp.int32, (1, slots), 1) < count_ref[0]
            target = jnp.where(live, places[1:2, :], -1.0).astype(jnp.int32)
            scatter_hot[...] = jnp.where(slot_id == target, 1.0, 0.0).astype(
                jnp.bfloat16
            )
        for step in range(2, lines):
            forward_line(step)
        for step in range(1, lines):
            forward_first(step)
        for copy in row_copies:
            copy.wait_recv()

        def middle(tile, carry, layer_id=layer_id):
            span = pl.ds(pl.multiple_of(tile * EDGE_ROWS, EDGE_ROWS), EDGE_ROWS)
            acc[span, :] += product(
                onehot[span, : 2 * group], table[layer_id, : 2 * group, :]
            ) + product(onehot[span, send_rows:], table[layer_id, send_rows:, :])
            return carry

        def third(tile, carry, layer_id=layer_id):
            span = pl.ds(pl.multiple_of(tile * EDGE_ROWS, EDGE_ROWS), EDGE_ROWS)
            acc[span, :] += product(
                onehot[span, 2 * group : 3 * group],
                table[layer_id, 2 * group : 3 * group, :],
            )
            return carry

        lax.fori_loop(0, tiles, middle, 0)
        for step in range(lines):
            for half in range(HALVES):
                copies[half, 2 * lines + step].wait_recv()
        lax.fori_loop(0, tiles, third, 0)
        for step in range(lines):
            for half in range(HALVES):
                copies[half, 3 * lines + step].wait_recv()

        loads["edge_out", layer_id].wait()
        partial_sum[...] = jnp.zeros_like(partial_sum)

        def late(tile, carry, layer_id=layer_id):
            span = pl.ds(pl.multiple_of(tile * EDGE_ROWS, EDGE_ROWS), EDGE_ROWS)
            first_out = acc[span, :] + product(
                onehot[span, 3 * group : send_rows], table[layer_id, 3 * group : send_rows, :]
            )
            hidden = silu(first_out).astype(jnp.bfloat16)
            if layer_id == 0:
                before = edge_half[span, :].astype(jnp.float32)
            else:
                before = edge_state[span, :]
            after = before + layer_norm(product(hidden, w_edge_out[layer_id]))
            after_half = after.astype(jnp.bfloat16)
            if layer_id < layers - 1:
                edge_state[span, :] = after
                edge_half[span, :] = after_half
            partial_sum[...] += product(scatter_hot[:, span], after_half)
            return carry

        lax.fori_loop(0, tiles, late, 0)

        part_copies = []
        for step in range(1, rows):
            part_out[layer_id, step - 1] = partial_sum[
                step * own : (step + 1) * own, :
            ].astype(jnp.bfloat16)
            copy = pltpu.make_async_remote_copy(
                src_ref=part_out.at[layer_id, step - 1],
                dst_ref=part_in.at[layer_id, step - 1],
                send_sem=part_send.at[layer_id, step - 1],
                recv_sem=part_recv.at[layer_id, step - 1],
                device_id={"row": row_peer(step)},
                device_id_type=MESH,
            )
            copy.start()
            part_copies.append(copy)
            pending.append(copy)
        edge_total = partial_sum[:own, :]
        for step, copy in enumerate(part_copies):
            copy.wait_recv()
            edge_total = edge_total + part_in[layer_id, step].astype(jnp.float32)

        loads["node_out", layer_id].wait()
        first_out = node_first[...] + product(
            edge_total.astype(jnp.bfloat16), w_node_in[layer_id, width:, :]
        )
        hidden = silu(first_out).astype(jnp.bfloat16)
        after = node_state[...] + layer_norm(product(hidden, w_node_out[layer_id]))
        if layer_id < layers - 1:
            node_state[...] = after
        else:
            out_ref[...] = after
    for copy in pending:
        copy.wait_send()


def per_device(
    node_latent, edge_latent, senders, receivers, edge_count, edge_in, edge_out, node_in, node_out
):
    own, width = node_latent.shape
    slots = edge_latent.shape[0]
    layers = edge_in.shape[0]
    cols = lax.axis_size("col")
    rows = lax.axis_size("row")
    lines = cols // 4
    send_rows, recv_rows = cols * own, rows * own
    half_type, full_type = jnp.bfloat16, jnp.float32
    vmem = pl.BlockSpec(memory_space=pltpu.VMEM)
    anywhere = pl.BlockSpec(memory_space=pl.ANY)
    dma = pltpu.SemaphoreType.DMA
    return pl.pallas_call(
        functools.partial(kernel, lines),
        out_shape=jax.ShapeDtypeStruct((own, width), full_type),
        in_specs=[pl.BlockSpec(memory_space=pltpu.SMEM)] + [vmem] * 2 + [anywhere] * 6,
        out_specs=vmem,
        scratch_shapes=[
            pltpu.VMEM((own, width), full_type),
            pltpu.VMEM((slots, width), half_type),
            pltpu.VMEM((slots, width), full_type),
            pltpu.VMEM((slots, width), full_type),
            pltpu.VMEM((slots, send_rows + recv_rows), half_type),
            pltpu.VMEM((recv_rows, slots), half_type),
            pltpu.VMEM((layers, send_rows + recv_rows, width), half_type),
            pltpu.VMEM(edge_in.shape, half_type),
            pltpu.VMEM(edge_out.shape, half_type),
            pltpu.VMEM(node_in.shape, half_type),
            pltpu.VMEM(node_out.shape, half_type),
            pltpu.VMEM((recv_rows, width), full_type),
            pltpu.VMEM((layers, rows - 1, own, width), half_type),
            pltpu.VMEM((layers, rows - 1, own, width), half_type),
            pltpu.VMEM((own, width), full_type),
            pltpu.VMEM((2, slots), full_type),
            dma((2 + 6 * layers,)),
            dma((layers, HALVES, cols)),
            dma((layers, HALVES, cols)),
            dma((layers, rows - 1)),
            dma((layers, rows - 1)),
            dma((layers, rows - 1)),
            dma((layers, rows - 1)),
        ],
        compiler_params=pltpu.CompilerParams(
            collective_id=0, has_side_effects=True, vmem_limit_bytes=60 * 1024 * 1024
        ),
    )(edge_count, senders[None, :], receivers[None, :], node_latent, edge_latent, edge_in, edge_out, node_in, node_out)


def solution(mesh):
    placed = (
        P(("row", "col"), None),
        P(("row", "col"), None),
        P(("row", "col")),
        P(("row", "col")),
        P(("row", "col")),
        P(),
        P(),
        P(),
        P(),
    )
    return jax.shard_map(
        per_device, mesh=mesh, in_specs=placed, out_specs=P(("row", "col"), None), check_vma=False
    )
```

```python
import functools

import jax
import jax.numpy as jnp
from jax import lax
from jax.experimental import pallas as pl
from jax.experimental.pallas import tpu as pltpu
from jax.sharding import PartitionSpec as P

MESH = pl.DeviceIdType.MESH
HALVES = 2
EDGE_ROWS = 1024
CHUNK = 128


def layer_norm(values):
    centre = values - jnp.mean(values, axis=-1, keepdims=True)
    spread = jnp.mean(centre * centre, axis=-1, keepdims=True)
    return centre * lax.rsqrt(spread + 1e-05)


def product(matrix, weight):
    return jnp.dot(matrix, weight, preferred_element_type=jnp.float32)


def silu(values):
    half = 0.5 * values
    return half + half * jnp.tanh(half)


def kernel(
    lines,
    count_ref,
    senders_ref,
    receivers_ref,
    node_hbm,
    edge_hbm,
    edge_in_hbm,
    edge_out_hbm,
    node_in_hbm,
    node_out_hbm,
    out_ref,
    node_state,
    edge_half,
    edge_state,
    acc,
    onehot,
    scatter_hot,
    table,
    w_edge_in,
    w_edge_out,
    w_node_in,
    w_node_out,
    partial_sum,
    part_out,
    part_in,
    node_first,
    places,
    load_sem,
    gather_send,
    gather_recv,
    row_send,
    row_recv,
    part_send,
    part_recv,
):
    layers, _, width = w_edge_in.shape
    own = node_state.shape[0]
    slots = edge_half.shape[0]
    rows = part_in.shape[1] + 1
    piece = own // HALVES
    group = HALVES * lines * piece
    send_rows = 4 * group
    recv_rows = rows * own
    tiles = slots // EDGE_ROWS

    row_me = lax.axis_index("row")
    col_me = lax.axis_index("col")
    a_me = col_me // 4
    inner = lax.rem(col_me, 4)
    b_me = inner // 2
    c_me = lax.rem(inner, 2)
    flip_b = a_me * 4 + (1 - b_me) * 2 + c_me
    flip_c = a_me * 4 + b_me * 2 + (1 - c_me)

    def line_peer(step):
        return lax.rem(a_me + lines - step, lines) * 4 + inner

    def row_peer(step):
        return lax.rem(row_me + rows + step, rows)

    barrier = pltpu.get_barrier_semaphore()
    for step in range(1, lines):
        pl.semaphore_signal(barrier, inc=1, device_id={"col": line_peer(step)}, device_id_type=MESH)
    for target in (flip_b, flip_c):
        pl.semaphore_signal(barrier, inc=1, device_id={"col": target}, device_id_type=MESH)
    for step in range(1, rows):
        pl.semaphore_signal(barrier, inc=1, device_id={"row": row_peer(step)}, device_id_type=MESH)

    loads = {}

    def load(name, source, target):
        copy = pltpu.make_async_copy(source, target, load_sem.at[len(loads)])
        copy.start()
        loads[name] = copy

    def load_edge_in(layer_id, name, part):
        span = pl.ds(part * width, width)
        load((name, layer_id), edge_in_hbm.at[layer_id, span], w_edge_in.at[layer_id, span])

    def load_rest():
        for layer_id in range(layers):
            if layer_id > 0:
                load_edge_in(layer_id, "send", 1)
            load_edge_in(layer_id, "receive", 2)
            load(("node_in", layer_id), node_in_hbm.at[layer_id], w_node_in.at[layer_id])
            load_edge_in(layer_id, "edge", 0)
            if layer_id == 0:
                load("edges", edge_hbm, edge_half)
            load(("edge_out", layer_id), edge_out_hbm.at[layer_id], w_edge_out.at[layer_id])
            load(("node_out", layer_id), node_out_hbm.at[layer_id], w_node_out.at[layer_id])

    load("node", node_hbm, node_state)
    load_edge_in(0, "send", 1)

    def floor_part(values, size):
        return jnp.floor((values + 0.5) * (1.0 / size))

    def place_edges():
        local = (senders_ref[...] - row_me * (own * 4 * lines)).astype(jnp.float32)
        block = floor_part(local, own)
        offset = local - block * own
        line = floor_part(block, 4)
        corner = block - line * 4
        corner_b = floor_part(corner, 2)
        line = line - a_me.astype(jnp.float32)
        line = jnp.where(line < 0.0, line + lines, line)
        flipped_b = jnp.abs(corner_b - b_me.astype(jnp.float32))
        flipped_c = jnp.abs(corner - corner_b * 2 - c_me.astype(jnp.float32))
        half = floor_part(offset, piece)
        first = jnp.where(half == 0.0, flipped_c, flipped_b)
        second = jnp.where(half == 0.0, flipped_b, flipped_c)
        places[0:1, :] = (
            (second * 2 + first) * group
            + half * (lines * piece)
            + line * piece
            + (offset - half * piece)
        )
        receiver = receivers_ref[...].astype(jnp.float32)
        patch = floor_part(receiver, own * 4 * lines)
        inside = receiver - patch * (own * 4 * lines)
        inside = inside - floor_part(inside, own) * own
        patch = patch - row_me.astype(jnp.float32)
        patch = jnp.where(patch < 0.0, patch + rows, patch)
        places[1:2, :] = patch * own + inside

    place_edges()

    def slot_row(half, slot):
        kind, line = slot // lines, slot % lines
        return kind * group + half * lines * piece + line * piece

    pending = []
    loads["node"].wait()
    for layer_id in range(layers):
        copies = {}

        def push(half, source, slot, target, layer_id=layer_id, copies=copies):
            copy = pltpu.make_async_remote_copy(
                src_ref=table.at[layer_id, pl.ds(slot_row(half, source), piece)],
                dst_ref=table.at[layer_id, pl.ds(slot_row(half, slot), piece)],
                send_sem=gather_send.at[layer_id, half, slot],
                recv_sem=gather_recv.at[layer_id, half, slot],
                device_id={"col": target},
                device_id_type=MESH,
            )
            copy.start()
            copies[half, slot] = copy
            pending.append(copy)

        first_target = (flip_c, flip_b)
        second_target = (flip_b, flip_c)
        w_edge = w_edge_in.at[layer_id]
        node_half = node_state[...].astype(jnp.bfloat16)

        loads["send", layer_id].wait()
        sent = product(node_half, w_edge[width : 2 * width, :]).astype(jnp.bfloat16)
        for half in range(HALVES):
            table[layer_id, pl.ds(slot_row(half, 0), piece), :] = sent[
                half * piece : (half + 1) * piece
            ]
        if layer_id == 0:
            pl.semaphore_wait(barrier, lines - 1 + 2 + rows - 1)
        for half in range(HALVES):
            push(half, 0, lines, first_target[half])
        for step in range(1, lines):
            for half in range(HALVES):
                push(half, 0, step, line_peer(step))
        for half in range(HALVES):
            push(half, 0, 2 * lines, second_target[half])
        if layer_id == 0:
            load_rest()

        loads["receive", layer_id].wait()
        table[layer_id, pl.ds(send_rows, own), :] = product(
            node_half, w_edge[2 * width : 3 * width, :]
        ).astype(jnp.bfloat16)
        row_copies = []
        for step in range(1, rows):
            copy = pltpu.make_async_remote_copy(
                src_ref=table.at[layer_id, pl.ds(send_rows, own)],
                dst_ref=table.at[layer_id, pl.ds(send_rows + step * own, own)],
                send_sem=row_send.at[layer_id, step - 1],
                recv_sem=row_recv.at[layer_id, step - 1],
                device_id={"row": row_peer(-step)},
                device_id_type=MESH,
            )
            copy.start()
            row_copies.append(copy)
            pending.append(copy)

        loads["node_in", layer_id].wait()
        node_first[...] = product(node_half, w_node_in[layer_id, :width, :])

        loads["edge", layer_id].wait()
        if layer_id == 0:
            loads["edges"].wait()

        def early(tile, carry, layer_id=layer_id, w_edge=w_edge):
            span = pl.ds(pl.multiple_of(tile * EDGE_ROWS, EDGE_ROWS), EDGE_ROWS)
            acc[span, :] = product(edge_half[span, :], w_edge[:width, :])
            if layer_id == 0:
                diagonal = lax.broadcasted_iota(
                    jnp.int32, (CHUNK, CHUNK), 0
                ) == lax.broadcasted_iota(jnp.int32, (CHUNK, CHUNK), 1)
                for chunk in range(EDGE_ROWS // CHUNK):
                    part = pl.ds(
                        pl.multiple_of(tile * EDGE_ROWS + chunk * CHUNK, CHUNK), CHUNK
                    )
                    for place, low, high in (
                        (0, 0, send_rows),
                        (1, send_rows, send_rows + recv_rows),
                    ):
                        column = jnp.sum(
                            jnp.where(diagonal, places[place : place + 1, part], 0.0),
                            axis=1,
                            keepdims=True,
                        ).astype(jnp.int32)
                        lane = lax.broadcasted_iota(jnp.int32, (CHUNK, high - low), 1)
                        onehot[part, low:high] = jnp.where(lane == column, 1.0, 0.0).astype(
                            jnp.bfloat16
                        )
            return carry

        def forward_line(step):
            for half in range(HALVES):
                copies[half, step].wait_recv()
                push(half, step, lines + step, first_target[half])
                push(half, step, 2 * lines + step, second_target[half])

        def forward_first(step):
            for half in range(HALVES):
                copies[half, lines + step].wait_recv()
                push(half, lines + step, 3 * lines + step, second_target[half])

        middle_tile = tiles // 2
        lax.fori_loop(0, middle_tile, early, 0)
        forward_first(0)
        forward_line(1)
        lax.fori_loop(middle_tile, tiles, early, 0)
        if layer_id == 0:
            slot_id = lax.broadcasted_iota(jnp.int32, (recv_rows, slots), 0)
            live = lax.broadcasted_iota(jnp.int32, (1, slots), 1) < count_ref[0]
            target = jnp.where(live, places[1:2, :], -1.0).astype(jnp.int32)
            scatter_hot[...] = jnp.where(slot_id == target, 1.0, 0.0).astype(
                jnp.bfloat16
            )
        for step in range(2, lines):
            forward_line(step)
        for step in range(1, lines):
            forward_first(step)
        for copy in row_copies:
            copy.wait_recv()

        def middle(tile, carry, layer_id=layer_id):
            span = pl.ds(pl.multiple_of(tile * EDGE_ROWS, EDGE_ROWS), EDGE_ROWS)
            acc[span, :] += product(
                onehot[span, : 2 * group], table[layer_id, : 2 * group, :]
            ) + product(onehot[span, send_rows:], table[layer_id, send_rows:, :])
            return carry

        def third(tile, carry, layer_id=layer_id):
            span = pl.ds(pl.multiple_of(tile * EDGE_ROWS, EDGE_ROWS), EDGE_ROWS)
            acc[span, :] += product(
                onehot[span, 2 * group : 3 * group],
                table[layer_id, 2 * group : 3 * group, :],
            )
            return carry

        lax.fori_loop(0, tiles, middle, 0)
        for step in range(lines):
            for half in range(HALVES):
                copies[half, 2 * lines + step].wait_recv()
        lax.fori_loop(0, tiles, third, 0)
        for step in range(lines):
            for half in range(HALVES):
                copies[half, 3 * lines + step].wait_recv()

        loads["edge_out", layer_id].wait()
        partial_sum[...] = jnp.zeros_like(partial_sum)

        def late(tile, carry, layer_id=layer_id):
            span = pl.ds(pl.multiple_of(tile * EDGE_ROWS, EDGE_ROWS), EDGE_ROWS)
            first_out = acc[span, :] + product(
                onehot[span, 3 * group : send_rows], table[layer_id, 3 * group : send_rows, :]
            )
            hidden = silu(first_out).astype(jnp.bfloat16)
            if layer_id == 0:
                before = edge_half[span, :].astype(jnp.float32)
            else:
                before = edge_state[span, :]
            after = before + layer_norm(product(hidden, w_edge_out[layer_id]))
            after_half = after.astype(jnp.bfloat16)
            if layer_id < layers - 1:
                edge_state[span, :] = after
                edge_half[span, :] = after_half
            partial_sum[...] += product(scatter_hot[:, span], after_half)
            return carry

        lax.fori_loop(0, tiles, late, 0, unroll=True)

        part_copies = []
        for step in range(1, rows):
            part_out[layer_id, step - 1] = partial_sum[
                step * own : (step + 1) * own, :
            ].astype(jnp.bfloat16)
            copy = pltpu.make_async_remote_copy(
                src_ref=part_out.at[layer_id, step - 1],
                dst_ref=part_in.at[layer_id, step - 1],
                send_sem=part_send.at[layer_id, step - 1],
                recv_sem=part_recv.at[layer_id, step - 1],
                device_id={"row": row_peer(step)},
                device_id_type=MESH,
            )
            copy.start()
            part_copies.append(copy)
            pending.append(copy)
        edge_total = partial_sum[:own, :]
        for step, copy in enumerate(part_copies):
            copy.wait_recv()
            edge_total = edge_total + part_in[layer_id, step].astype(jnp.float32)

        loads["node_out", layer_id].wait()
        first_out = node_first[...] + product(
            edge_total.astype(jnp.bfloat16), w_node_in[layer_id, width:, :]
        )
        hidden = silu(first_out).astype(jnp.bfloat16)
        after = node_state[...] + layer_norm(product(hidden, w_node_out[layer_id]))
        if layer_id < layers - 1:
            node_state[...] = after
        else:
            out_ref[...] = after
    for copy in pending:
        copy.wait_send()


def per_device(
    node_latent, edge_latent, senders, receivers, edge_count, edge_in, edge_out, node_in, node_out
):
    own, width = node_latent.shape
    slots = edge_latent.shape[0]
    layers = edge_in.shape[0]
    cols = lax.axis_size("col")
    rows = lax.axis_size("row")
    lines = cols // 4
    send_rows, recv_rows = cols * own, rows * own
    half_type, full_type = jnp.bfloat16, jnp.float32
    vmem = pl.BlockSpec(memory_space=pltpu.VMEM)
    anywhere = pl.BlockSpec(memory_space=pl.ANY)
    dma = pltpu.SemaphoreType.DMA
    return pl.pallas_call(
        functools.partial(kernel, lines),
        out_shape=jax.ShapeDtypeStruct((own, width), full_type),
        in_specs=[pl.BlockSpec(memory_space=pltpu.SMEM)] + [vmem] * 2 + [anywhere] * 6,
        out_specs=vmem,
        scratch_shapes=[
            pltpu.VMEM((own, width), full_type),
            pltpu.VMEM((slots, width), half_type),
            pltpu.VMEM((slots, width), full_type),
            pltpu.VMEM((slots, width), full_type),
            pltpu.VMEM((slots, send_rows + recv_rows), half_type),
            pltpu.VMEM((recv_rows, slots), half_type),
            pltpu.VMEM((layers, send_rows + recv_rows, width), half_type),
            pltpu.VMEM(edge_in.shape, half_type),
            pltpu.VMEM(edge_out.shape, half_type),
            pltpu.VMEM(node_in.shape, half_type),
            pltpu.VMEM(node_out.shape, half_type),
            pltpu.VMEM((recv_rows, width), full_type),
            pltpu.VMEM((layers, rows - 1, own, width), half_type),
            pltpu.VMEM((layers, rows - 1, own, width), half_type),
            pltpu.VMEM((own, width), full_type),
            pltpu.VMEM((2, slots), full_type),
            dma((2 + 6 * layers,)),
            dma((layers, HALVES, cols)),
            dma((layers, HALVES, cols)),
            dma((layers, rows - 1)),
            dma((layers, rows - 1)),
            dma((layers, rows - 1)),
            dma((layers, rows - 1)),
        ],
        compiler_params=pltpu.CompilerParams(
            collective_id=0, has_side_effects=True, vmem_limit_bytes=60 * 1024 * 1024
        ),
    )(edge_count, senders[None, :], receivers[None, :], node_latent, edge_latent, edge_in, edge_out, node_in, node_out)


def solution(mesh):
    placed = (
        P(("row", "col"), None),
        P(("row", "col"), None),
        P(("row", "col")),
        P(("row", "col")),
        P(("row", "col")),
        P(),
        P(),
        P(),
        P(),
    )
    return jax.shard_map(
        per_device, mesh=mesh, in_specs=placed, out_specs=P(("row", "col"), None), check_vma=False
    )
```
